32 devices in a mesh: aa: 4 (over x, core), ba: 2 (over y), col: 4 (over z).
Axes of the slice: x: 2, y: 2, z: 4, core: 2. Of those that a mesh axis runs over, the one named last changes fastest.
Arguments:
- field: float32 [96, 1024, 1024], P('col', 'aa', 'ba'), may hold values from -6 to 6
- factor: float32 [1024, 256], P('aa'), may hold values from -0.1875 to 0.1875
Outputs:
- gram: float32 [1024, 1024], P('ba', ('aa', 'col'))
The draws below stay inside these ranges and needn't reach their ends.
All inputs are finite; a program needn't handle non-finite values.
Results may differ from the reference program's by a relative error of at most 0.000076.
Values sent between devices are 32-bit elements; how exact they have to be, the bound alone decides.
No kernel may reach another device: no remote copies, remote signals or barrier semaphores. Data moves between devices by JAX's collectives and lax.ppermute only.
A program may use at most 64 MiB of HBM per device.

```python
import jax
import jax.numpy as jnp
from jax import lax

N1 = 1024
N2 = 1024
R1 = 256
NZ = 96


def level_of(key, extent, shards, low, largest):
    def one(dim, shards_of):
        draws = jax.random.uniform(jax.random.fold_in(jax.random.fold_in(key, 6), dim), (shards_of,), jnp.float32, low / len(shards), largest / len(shards))
        return jnp.repeat(jnp.exp(draws), extent[dim] // shards_of).reshape((-1,) + (1,) * (len(extent) - dim - 1))

    level = one(*shards[0])
    for cut in shards[1:]:
        level = level * one(*cut)
    return level


def noise(rng, shape, spread, reach, split=(), held_as=jnp.bfloat16):
    factor_of = level_of(rng, shape, split, -0.22, 0.18) if split else 1.0
    entries = jax.random.normal(rng, shape, jnp.float32) * spread * factor_of
    return jnp.minimum(jnp.maximum(entries, -reach), reach).astype(held_as)


def setup_inputs(seed: int = 0) -> dict:
    splits = jax.random.split(jax.random.key(seed), 3)
    return {
        "field": noise(splits[0], (NZ, N1, N2), 1.0, 6.0, ((0, 4), (1, 4), (2, 2)), jnp.float32),
        "factor": noise(splits[1], (N1, R1), N1 ** -0.5, 0.1875, ((0, 4),), jnp.float32),
    }


def reference(field, factor):
    core = jnp.einsum('kab,ar->krb', field, factor, precision=lax.Precision.HIGHEST)
    gram = jnp.einsum('krb,krc->bc', core, core, precision=lax.Precision.HIGHEST)
    return gram / jnp.sqrt(jnp.float32(R1 * NZ))
```

```python
import jax
import jax.numpy as jnp
from jax import lax
from jax.sharding import PartitionSpec as P

MULTIPLY = lax.Precision.HIGH


def swap(x, axis, bit):
    size = lax.axis_size(axis)
    return lax.ppermute(x, axis, [(i, i ^ bit) for i in range(size)])


def bits_of(size):
    return [1 << n for n in range(size.bit_length() - 1)]


def summed_over_aa(parts, bits):
    for bit in bits:
        kept = {d: p for d, p in parts.items() if not d & bit}
        for d in reversed(sorted(kept)):
            kept[d] = kept[d] + swap(parts[d | bit], "aa", bit)
        parts = kept
    return parts[0]


def shards(field, factor):
    aa, ba, col = (lax.axis_size(n) for n in ("aa", "ba", "col"))
    me_a, me_b, me_c = (lax.axis_index(n) for n in ("aa", "ba", "col"))
    ranks = factor.shape[1]
    depth = field.shape[0] * col
    each = field.shape[0] // aa
    width = field.shape[2]
    gram = jnp.zeros((ba * width, width), jnp.float32)
    for step in range(each):
        terms = {}
        for d in reversed(range(aa)):
            layer = lax.dynamic_index_in_dim(field, (me_a ^ d) * each + step, 0, keepdims=False)
            terms[d] = jnp.einsum("ab,ar->rb", layer, factor, precision=MULTIPLY)
        core = summed_over_aa(terms, bits_of(aa))
        others = {0: core}
        for d in range(1, ba):
            others[d] = swap(core, "ba", d)
        stacked = jnp.stack([others[d] for d in range(ba)])
        ordered = jnp.concatenate(
            [lax.dynamic_index_in_dim(stacked, me_b ^ y, 0, keepdims=False) for y in range(ba)], axis=1
        )
        gram = gram + jnp.einsum("rc,rb->cb", ordered, core, precision=MULTIPLY)
    rest = ba * width // (aa * col)
    gram = gram.reshape(aa, col, rest, width)
    pieces = {d: lax.dynamic_index_in_dim(gram, me_a ^ d, 0, keepdims=False) for d in range(aa)}
    low = {d: pieces[d] + swap(pieces[d | 1], "aa", 1) for d in pieces if not d & 1}
    tall = jnp.stack([low[d] for d in sorted(low)], axis=1)
    total = lax.dynamic_index_in_dim(tall, me_c, 0, keepdims=False)
    for d in range(1, col):
        total = total + swap(lax.dynamic_index_in_dim(tall, me_c ^ d, 0, keepdims=False), "col", d)
    mine = summed_over_aa({d: total[n] for n, d in enumerate(sorted(low))}, bits_of(aa)[1:])
    return mine.T / jnp.sqrt(jnp.float32(ranks * depth))


def solution(mesh):
    placed = (P("col", "aa", "ba"), P("aa", None))
    return jax.shard_map(
        shards, mesh=mesh, in_specs=placed, out_specs=P("ba", ("aa", "col")), check_vma=False
    )
```

```python
import functools

import jax
import jax.numpy as jnp
from jax import lax
from jax.experimental import pallas as pl
from jax.experimental.pallas import tpu as pltpu
from jax.sharding import PartitionSpec as P

VMEM_LIMIT = 48 << 20
LAG = 3


def swap(x, axis, bit):
    return lax.ppermute(x, axis, [(i, i ^ bit) for i in range(lax.axis_size(axis))])


def tie(x, *after):
    return lax.optimization_barrier((x, *after))[0]


def split(x):
    high = x.astype(jnp.bfloat16)
    return high, (x - high.astype(jnp.float32)).astype(jnp.bfloat16)


def product(a, b, dims):
    dot = functools.partial(lax.dot_general, dimension_numbers=(dims, ((), ())), preferred_element_type=jnp.float32)
    return dot(a[0], b[0]) + (dot(a[0], b[1]) + dot(a[1], b[0]))


def truncate_kernel(_, layer_ref, factor_ref, out_ref):
    out_ref[0] = product(split(layer_ref[0]), split(factor_ref[...]), ((0,), (0,)))


def truncated(layers, field, factor):
    count = layers.shape[0]
    _, rows, width = field.shape
    ranks = factor.shape[1]
    return pl.pallas_call(
        truncate_kernel,
        grid_spec=pltpu.PrefetchScalarGridSpec(
            num_scalar_prefetch=1,
            grid=(count,),
            in_specs=[
                pl.BlockSpec((1, rows, width), lambda i, n: (n[i], 0, 0)),
                pl.BlockSpec((rows, ranks), lambda i, n: (0, 0)),
            ],
            out_specs=pl.BlockSpec((1, width, ranks), lambda i, n: (i, 0, 0)),
        ),
        out_shape=jax.ShapeDtypeStruct((count, width, ranks), jnp.float32),
        compiler_params=pltpu.CompilerParams(vmem_limit_bytes=VMEM_LIMIT),
        cost_estimate=pl.CostEstimate(
            flops=6 * count * rows * width * ranks, bytes_accessed=4 * count * width * (rows + ranks), transcendentals=0
        ),
    )(layers, field, factor)


def gram_kernel(ba, widths, counts, unit, added, me_ref, *refs):
    strips, total = len(widths), ba * sum(counts)
    pieces, out_ref = refs[:total], refs[-1]
    old_ref = refs[total] if added else None
    owners, ranks = pieces[0].shape[1], pieces[0].shape[3]

    def pair(d, i):
        first = d * sum(counts) + sum(counts[:i])
        found = []
        for piece in pieces[first : first + counts[i]]:
            found += [split(piece[k].reshape(owners * widths[i], ranks)) for k in range(piece.shape[0])]
        return tuple(jnp.concatenate([x[n] for x in found], axis=1) for n in range(2))

    def put(block, row, size, value):
        value = value.reshape(owners, size, owners * unit)
        if added:
            value = value + old_ref[block, :, row : row + size, :]
        out_ref[block, :, row : row + size, :] = value

    pairs = {(d, i): pair(d, i) for d in range(ba) for i in range(strips)}
    lanes, wide = owners * unit, widths[-1]
    for d in range(ba):
        block = me_ref[0] ^ d
        row = 0
        for i, w in enumerate(widths):
            got = product(pairs[d, strips - 1], pairs[0, i], ((1,), (1,)))
            for n in range(w // unit):
                put(block, row, wide, got[:, n * lanes : (n + 1) * lanes])
                row += wide
        for n in range(wide // unit):
            mine = tuple(x[n * lanes : (n + 1) * lanes, :] for x in pairs[0, strips - 1])
            for i, w in enumerate(widths[:-1]):
                put(block, row, w, product(pairs[d, i], mine, ((1,), (1,))))
                row += w


def gram_strip(me, pieces, widths, unit, old):
    ba, counts = len(pieces), [len(x) for x in pieces[0]]
    owners, ranks = pieces[0][0][0].shape[1], pieces[0][0][0].shape[3]
    rows = (sum(widths) * widths[-1] + sum(widths[:-1]) * widths[-1]) // unit
    flat = [x for by_strip in pieces for by_chunk in by_strip for x in by_chunk]
    inner = ranks * sum(x.shape[0] for x in pieces[0][0])
    olds = [] if old is None else [old]
    full = pl.BlockSpec(memory_space=pltpu.VMEM)
    return pl.pallas_call(
        functools.partial(gram_kernel, ba, widths, counts, unit, len(olds)),
        in_specs=[pl.BlockSpec(memory_space=pltpu.SMEM)] + [full] * (len(flat) + len(olds)),
        out_specs=full,
        out_shape=jax.ShapeDtypeStruct((ba, owners, rows, owners * unit), jnp.float32),
        input_output_aliases={1 + len(flat): 0} if olds else {},
        compiler_params=pltpu.CompilerParams(vmem_limit_bytes=VMEM_LIMIT),
        cost_estimate=pl.CostEstimate(
            flops=6 * ba * owners * owners * rows * unit * inner, bytes_accessed=4 * sum(x.size for x in flat), transcendentals=0
        ),
    )(me.reshape(1).astype(jnp.int32), *flat, *olds)


def order_of(bits):
    if not bits:
        return [0]
    rest = order_of(bits[1:])
    return [d | bits[0] for d in rest] + rest


def strips_of(rest):
    widths = []
    while rest > 16 and rest % 2 == 0 and len(widths) < 2:
        rest //= 2
        widths.append(rest)
    return widths + [rest]


def summed_over_core(region):
    aa = region.shape[0]
    core = lax.axis_index("aa") & 1
    pairs = region.reshape(aa // 2, 2, *region.shape[1:])
    send = lax.dynamic_index_in_dim(pairs, core ^ 1, 1, keepdims=False)
    return lax.dynamic_index_in_dim(pairs, core, 1, keepdims=False) + swap(send, "aa", 1)


def block_by_permutes(region):
    t = summed_over_core(region)
    me_x, me_c = lax.axis_index("aa") >> 1, lax.axis_index("col")
    total = lax.dynamic_index_in_dim(t, me_c, 1, keepdims=False)
    for d in range(1, region.shape[1]):
        total = total + swap(lax.dynamic_index_in_dim(t, me_c ^ d, 1, keepdims=False), "col", d)
    places = total.shape[0]
    mine = lax.dynamic_index_in_dim(total, me_x, 0, keepdims=False)
    for d in range(1, places):
        mine = mine + swap(lax.dynamic_index_in_dim(total, me_x ^ d, 0, keepdims=False), "aa", 2 * d)
    return mine


def block_by_all_to_all(region):
    aa, col = region.shape[:2]
    t = summed_over_core(region)
    groups = [[(x * 2 + c) * col + z for x in range(aa // 2) for z in range(col)] for c in range(2)]
    t = t.reshape(aa // 2 * col, *t.shape[2:])
    return jnp.sum(lax.all_to_all(t, ("aa", "col"), 0, 0, tiled=True, axis_index_groups=groups), axis=0)


def shards(field, factor):
    aa, ba, col = (lax.axis_size(n) for n in ("aa", "ba", "col"))
    me_a, me_b = lax.axis_index("aa"), lax.axis_index("ba")
    ranks, width = factor.shape[1], field.shape[2]
    depth = field.shape[0] * col
    each = field.shape[0] // aa
    rest = ba * width // (aa * col)
    owners = width // rest
    widths = strips_of(rest)
    unit = widths[-1]
    bits = [1 << n for n in range(aa.bit_length() - 1)]
    keep = order_of(bits[1:])
    send = [d | 1 for d in keep]

    def layers(places, c):
        return jnp.concatenate([((me_a ^ d) * each + c).reshape(1) for d in places])

    def groups_of(i):
        size = 1 if i == 0 else 2 if each % 2 == 0 else 1
        return [range(c, c + size) for c in range(0, each, size)]

    def parts_of(c, i):
        first = sum(widths[:i])
        kept, came = kept_of[c], came_of[c]
        kept, came = (x.reshape(len(keep), 1, owners, rest, ranks)[:, :, :, first : first + widths[i]] for x in (kept, came))
        return kept + came

    kept_of, came_of = {}, {}

    def send_core(c, *after):
        out = truncated(tie(layers(send, c), *after), field, factor)
        came_of[c] = swap(out, "aa", 1)
        return out

    def keep_core(c, *after):
        kept_of[c] = truncated(tie(layers(keep, c), *after), field, factor)

    steps = [(i, group) for i in range(len(widths)) for group in groups_of(i)]
    pieces = {}
    regions, blocks = [None] * len(widths), []
    arrived, passed, waiting, leaving_of = [], [], [], {}

    def add_gram(i, group, *after):
        used = [
            [[pieces[d, s, g] for g in groups_of(s) if g[0] in group] for s in range(i + 1)] for d in range(ba)
        ]
        regions[i] = gram_strip(tie(me_b, *after), used, widths[: i + 1], unit, regions[i])
        if group[-1] == each - 1:
            region = regions[i].reshape(aa, col, *regions[i].shape[2:])
            blocks.append(block_by_permutes(region) if i < len(widths) - 1 else block_by_all_to_all(region))

    keep_core(0, send_core(0))
    out = send_core(1, kept_of[0]) if each > 1 else None
    for n, (i, group) in enumerate(steps):
        t = jnp.concatenate([parts_of(c, i) for c in group], axis=1)
        half = t.shape[0] // 2
        leaving, t = (t[:half], t[half:]) if bits[1:] else (t, t)
        if i == 0 and n + 1 < each:
            keep_core(n + 1, leaving, out)
            if n + 2 < each:
                out = send_core(n + 2, kept_of[n + 1])
        after = ([arrived[n - 2]] if n >= 2 else []) + (passed[n - 4] if n >= 4 else [])
        if after:
            leaving = tie(leaving, *after)
        leaving_of[n] = leaving
        for bit in bits[1:]:
            t = t + swap(leaving, "aa", bit)
            half = t.shape[0] // 2
            leaving, t = (t[:half], t[half:]) if half else (t, t)
        t = t[0]
        arrived.append(t)
        passed.append([swap(t, "ba", d) for d in range(1, ba)])
        for d, x in enumerate([t] + passed[-1]):
            pieces[d, i, group] = x
        waiting.append((i, group))
        if len(waiting) > LAG:
            add_gram(*waiting.pop(0), leaving_of[n])
    while waiting:
        add_gram(*waiting.pop(0))

    lanes = owners * unit
    columns = [[None] * len(widths) for _ in widths]
    for j, wide in enumerate(widths):
        row = 0
        for i in range(j + 1):
            n = widths[i] // unit
            columns[i][j] = blocks[j][row : row + n * wide].reshape(n, wide, lanes).swapaxes(1, 2).reshape(n * lanes, wide)
            row += n * wide
        n, before = wide // unit, sum(widths[:j])
        if j:
            earlier = blocks[j][row:].reshape(n, before, lanes).swapaxes(1, 2).reshape(n * lanes, before)
            for i in range(j):
                at = sum(widths[:i])
                columns[j][i] = earlier[:, at : at + widths[i]]
    parts = [jnp.concatenate(columns[i], axis=1).reshape(owners, widths[i], rest) for i in range(len(widths))]
    return jnp.concatenate(parts, axis=1).reshape(width, rest) / jnp.sqrt(jnp.float32(ranks * depth))


def solution(mesh):
    placed = (P("col", "aa", "ba"), P("aa", None))
    return jax.shard_map(
        shards, mesh=mesh, in_specs=placed, out_specs=P("ba", ("aa", "col")), check_vma=False
    )
```

```python
import functools
import math

import jax
import jax.numpy as jnp
from jax import lax
from jax.experimental import pallas as pl
from jax.experimental.pallas import tpu as pltpu
from jax.sharding import PartitionSpec as P

VMEM_LIMIT = 48 << 20
LAG = 2
DEEP = 3
BRIEF = pl.CostEstimate(flops=0, bytes_accessed=0, transcendentals=0)


def swap(x, axis, bit):
    return lax.ppermute(x, axis, [(i, i ^ bit) for i in range(lax.axis_size(axis))])


def tie(x, *after):
    return lax.optimization_barrier((x, *after))[0]


def split(x):
    high = x.astype(jnp.bfloat16)
    return high, (x - high.astype(jnp.float32)).astype(jnp.bfloat16)


def product(a, b, dims):
    dot = functools.partial(lax.dot_general, dimension_numbers=(dims, ((), ())), preferred_element_type=jnp.float32)
    return dot(a[0], b[0]) + (dot(a[0], b[1]) + dot(a[1], b[0]))


def gather_kernel(layers_ref, field_ref, out_ref, held, sems):
    count = out_ref.shape[0]
    reads = [pltpu.make_async_copy(field_ref.at[layers_ref[n]], held.at[n], sems.at[0, n]) for n in range(count)]
    writes = [pltpu.make_async_copy(held.at[n], out_ref.at[n], sems.at[1, n]) for n in range(count)]
    for read in reads:
        read.start()
    for read, write in zip(reads, writes):
        read.wait()
        write.start()
    for write in writes:
        write.wait()


def gathered(layers, field):
    shape = (layers.shape[0], *field.shape[1:])
    return pl.pallas_call(
        gather_kernel,
        in_specs=[pl.BlockSpec(memory_space=pltpu.SMEM), pl.BlockSpec(memory_space=pl.ANY)],
        out_specs=pl.BlockSpec(memory_space=pl.ANY),
        out_shape=jax.ShapeDtypeStruct(shape, field.dtype),
        scratch_shapes=[pltpu.VMEM(shape, field.dtype), pltpu.SemaphoreType.DMA((2, shape[0]))],
        compiler_params=pltpu.CompilerParams(vmem_limit_bytes=VMEM_LIMIT),
        cost_estimate=BRIEF,
    )(layers, field)


def truncate_kernel(cuts, _, *refs):
    own, came, own_factor, came_factor = refs[:4]
    layer = jnp.concatenate([own[0], came[0]], axis=0)
    factor = jnp.concatenate([own_factor[...], came_factor[...]], axis=0)
    out = product(split(layer), split(factor), ((0,), (0,)))
    owners = refs[4].shape[1]
    out = out.reshape(owners, -1, out.shape[1])
    for ref, (low, high) in zip(refs[4:], cuts):
        ref[0] = out[:, low:high]


def truncated(layers, slots, field, came, factors, owners, cuts):
    count = layers.shape[0]
    _, rows, width = field.shape
    ranks = factors[0].shape[1]
    outs = [(owners, high - low, ranks) for low, high in cuts]
    return pl.pallas_call(
        functools.partial(truncate_kernel, cuts),
        grid_spec=pltpu.PrefetchScalarGridSpec(
            num_scalar_prefetch=1,
            grid=(count,),
            in_specs=[
                pl.BlockSpec((1, rows, width), lambda i, n: (n[i], 0, 0)),
                pl.BlockSpec((1, rows, width), lambda i, n: (n[count + i], 0, 0)),
                pl.BlockSpec((rows, ranks), lambda i, n: (0, 0)),
                pl.BlockSpec((rows, ranks), lambda i, n: (0, 0)),
            ],
            out_specs=[pl.BlockSpec((1, *x), lambda i, n: (i, 0, 0, 0)) for x in outs],
        ),
        out_shape=[jax.ShapeDtypeStruct((count, *x), jnp.float32) for x in outs],
        compiler_params=pltpu.CompilerParams(vmem_limit_bytes=VMEM_LIMIT),
        cost_estimate=BRIEF,
    )(jnp.concatenate([layers, slots]), field, came, *factors)


def gram_kernel(ba, widths, counts, unit, added, me_ref, *refs):
    strips, total = len(widths), ba * sum(counts)
    pieces, out_ref = refs[:total], refs[-1]
    old_ref = refs[total] if added else None
    owners, ranks = pieces[0].shape[1], pieces[0].shape[3]

    def pair(d, i):
        first = d * sum(counts) + sum(counts[:i])
        found = []
        for piece in pieces[first : first + counts[i]]:
            found += [split(piece[k].reshape(owners * widths[i], ranks)) for k in range(piece.shape[0])]
        return tuple(jnp.concatenate([x[n] for x in found], axis=1) for n in range(2))

    def put(block, row, size, value):
        value = value.reshape(owners, size, owners * unit)
        if added:
            value = value + old_ref[block, :, row : row + size, :]
        out_ref[block, :, row : row + size, :] = value

    pairs = {(d, i): pair(d, i) for d in range(ba) for i in range(strips)}
    lanes, wide = owners * unit, widths[-1]
    for d in range(ba):
        block = me_ref[0] ^ d
        row = 0
        for i, w in enumerate(widths):
            got = product(pairs[d, strips - 1], pairs[0, i], ((1,), (1,)))
            for n in range(w // unit):
                put(block, row, wide, got[:, n * lanes : (n + 1) * lanes])
                row += wide
        for n in range(wide // unit):
            mine = tuple(x[n * lanes : (n + 1) * lanes, :] for x in pairs[0, strips - 1])
            for i, w in enumerate(widths[:-1]):
                put(block, row, w, product(pairs[d, i], mine, ((1,), (1,))))
                row += w


def gram_strip(me, pieces, widths, unit, old):
    ba, counts = len(pieces), [len(x) for x in pieces[0]]
    owners, ranks = pieces[0][0][0].shape[1], pieces[0][0][0].shape[3]
    rows = (sum(widths) * widths[-1] + sum(widths[:-1]) * widths[-1]) // unit
    flat = [x for by_strip in pieces for by_chunk in by_strip for x in by_chunk]
    inner = ranks * sum(x.shape[0] for x in pieces[0][0])
    olds = [] if old is None else [old]
    full = pl.BlockSpec(memory_space=pltpu.VMEM)
    return pl.pallas_call(
        functools.partial(gram_kernel, ba, widths, counts, unit, len(olds)),
        in_specs=[pl.BlockSpec(memory_space=pltpu.SMEM)] + [full] * (len(flat) + len(olds)),
        out_specs=full,
        out_shape=jax.ShapeDtypeStruct((ba, owners, rows, owners * unit), jnp.float32),
        input_output_aliases={1 + len(flat): 0} if olds else {},
        compiler_params=pltpu.CompilerParams(vmem_limit_bytes=VMEM_LIMIT),
        cost_estimate=BRIEF,
    )(me.reshape(1).astype(jnp.int32), *flat, *olds)


def order_of(bits):
    if not bits:
        return [0]
    rest = order_of(bits[1:])
    return [d | bits[0] for d in rest] + rest


def strips_of(rest):
    widths = []
    while rest > 16 and rest % 2 == 0 and len(widths) < 2:
        rest //= 2
        widths.append(rest)
    return widths + [rest]


def summed_over_core(region):
    aa = region.shape[0]
    core = lax.axis_index("aa") & 1
    pairs = region.reshape(aa // 2, 2, *region.shape[1:])
    send = lax.dynamic_index_in_dim(pairs, core ^ 1, 1, keepdims=False)
    return lax.dynamic_index_in_dim(pairs, core, 1, keepdims=False) + swap(send, "aa", 1)


def block_by_permutes(t):
    me_x, me_c = lax.axis_index("aa") >> 1, lax.axis_index("col")
    bit = t.shape[1] // 2
    while bit:
        halves = t.reshape(t.shape[0], 2, bit, *t.shape[2:])
        side = (me_c // bit) & 1
        leaving = lax.dynamic_index_in_dim(halves, side ^ 1, 1, keepdims=False)
        t = lax.dynamic_index_in_dim(halves, side, 1, keepdims=False) + swap(leaving, "col", bit)
        bit //= 2
    total = t[:, 0]
    places = total.shape[0]
    mine = lax.dynamic_index_in_dim(total, me_x, 0, keepdims=False)
    for d in range(1, places):
        mine = mine + swap(lax.dynamic_index_in_dim(total, me_x ^ d, 0, keepdims=False), "aa", 2 * d)
    return mine


def block_by_all_to_all(t):
    aa, col = 2 * t.shape[0], t.shape[1]
    groups = [[(x * 2 + c) * col + z for x in range(aa // 2) for z in range(col)] for c in range(2)]
    t = t.reshape(aa // 2 * col, *t.shape[2:])
    return jnp.sum(lax.all_to_all(t, ("aa", "col"), 0, 0, tiled=True, axis_index_groups=groups), axis=0)


def shards(field, factor):
    aa, ba, col = (lax.axis_size(n) for n in ("aa", "ba", "col"))
    me_a, me_b = lax.axis_index("aa"), lax.axis_index("ba")
    ranks, width = factor.shape[1], field.shape[2]
    depth = field.shape[0] * col
    each = field.shape[0] // aa
    rest = ba * width // (aa * col)
    owners = width // rest
    widths = strips_of(rest)
    unit = widths[-1]
    bits = [1 << n for n in range(aa.bit_length() - 1)]
    keep = order_of(bits[1:])
    middle = each // 2
    halves = [range(middle), range(middle, each)] if middle else [range(each)]

    def groups_of(i):
        if i == 0:
            return [range(c, c + 1) for c in range(each)]
        if i == len(widths) - 1 and len(halves[-1]) > 1:
            return halves[:-1] + [range(middle, each - 1), range(each - 1, each)]
        return halves

    cuts = [(0, widths[0])] + ([(widths[0], rest)] if len(widths) > 1 else [])
    trips = [range(c, c + 1) for c in range(min(2, each))] + ([range(2, each)] if each > 2 else [])
    came_of, terms = {}, {}
    factors = [factor, swap(factor, "aa", 1)]
    for n, trip in enumerate(trips):
        first = (me_a & 1 ^ 1) * each
        if n:
            first = tie(first, going, *(factors[1:] if n == 1 else []))
        going = gathered(jnp.stack([first + 2 * each * x + c for x in range(aa // 2) for c in trip]), field)
        if n > 1:
            going = tie(going, came_of[0][0])
        came = swap(going, "aa", 1)
        for c in trip:
            came_of[c] = came, [(me_a ^ d) // 2 * len(trip) + c - trip[0] for d in keep]

    def truncate(c, *after):
        came, slots = came_of[c]
        half = len(keep) // 2
        terms[c] = []
        for part in (range(half), range(half, len(keep))):
            if part:
                layers = jnp.stack([(me_a ^ keep[n]) * each + c for n in part])
                places = jnp.stack([slots[n] for n in part])
                after = tie(layers, *after), places
                terms[c].append(truncated(*after, field, came, factors, owners, cuts))
                after = terms[c][-1][:1]

    def terms_of(part, group, i):
        cut = min(i, 1)
        first = sum(widths[:i]) - cuts[cut][0]
        found = [terms[c][part][cut] for c in group]
        found = [x.reshape(x.shape[0], 1, *x.shape[1:])[:, :, :, first : first + widths[i]] for x in found]
        return jnp.concatenate(found, axis=1)

    steps = [(i, group) for i in range(len(widths)) for group in groups_of(i)]
    pieces = {}
    regions, blocks = [None] * len(widths), []
    arrived, passed, waiting, halfway, leaving_of = [], [], [], [], {}

    def add_gram(i, group, *after):
        used = [
            [[pieces[d, s, g] for g in groups_of(s) if g[0] in group] for s in range(i + 1)] for d in range(ba)
        ]
        regions[i] = gram_strip(tie(me_b, *after, *halfway), used, widths[: i + 1], unit, regions[i])
        if group[-1] == each - 1:
            region = regions[i].reshape(aa, col, *regions[i].shape[2:])
            summed = summed_over_core(region)
            halfway.append(summed)
            blocks.append(block_by_permutes(summed) if i < len(widths) - 1 else block_by_all_to_all(summed))

    def send(n):
        i, group = steps[n]
        if i == 0:
            truncate(n, *(terms[n - 1][-1][:1] if n else []), *(arrived[n - DEEP : n - DEEP + 1] if n >= DEEP else []))
        after = ([arrived[n - DEEP]] if n >= DEEP else []) + (passed[n - DEEP - 2] if n >= DEEP + 2 else [])
        leaving_of[n] = terms_of(0, group, i)
        if after:
            leaving_of[n] = tie(leaving_of[n], *after)

    for n in range(min(DEEP - 1, len(steps))):
        send(n)
    for n, (i, group) in enumerate(steps):
        ahead = n + DEEP - 1
        if ahead < len(steps):
            send(ahead)
        leaving = leaving_of[n]
        t = tie(terms_of(-1, group, i), leaving_of[min(ahead, len(steps) - 1)])
        for bit in bits[1:]:
            t = t + swap(leaving, "aa", bit)
            half = t.shape[0] // 2
            leaving, t = (t[:half], t[half:]) if half else (t, t)
        t = t[0]
        arrived.append(t)
        passed.append([swap(t, "ba", d) for d in range(1, ba)])
        for d, x in enumerate([t] + passed[-1]):
            pieces[d, i, group] = x
        for part in halves:
            if group[-1] == part[-1]:
                waiting.append((n, i, part))
        if waiting and waiting[0][0] <= n - LAG:
            add_gram(*waiting.pop(0)[1:], leaving_of[min(ahead, len(steps) - 1)])
    while waiting:
        add_gram(*waiting.pop(0)[1:])

    lanes = owners * unit
    columns = [[None] * len(widths) for _ in widths]
    for j, wide in enumerate(widths):
        row = 0
        for i in range(j + 1):
            n = widths[i] // unit
            columns[i][j] = blocks[j][row : row + n * wide].reshape(n, wide, lanes).swapaxes(1, 2).reshape(n * lanes, wide)
            row += n * wide
        n, before = wide // unit, sum(widths[:j])
        if j:
            earlier = blocks[j][row:].reshape(n, before, lanes).swapaxes(1, 2).reshape(n * lanes, before)
            for i in range(j):
                at = sum(widths[:i])
                columns[j][i] = earlier[:, at : at + widths[i]]
    parts = [jnp.concatenate(columns[i], axis=1).reshape(owners, widths[i], rest) for i in range(len(widths))]
    return jnp.concatenate(parts, axis=1).reshape(width, rest) / jnp.sqrt(jnp.float32(ranks * depth))


def solution(mesh):
    placed = (P("col", "aa", "ba"), P("aa", None))
    return jax.shard_map(
        shards, mesh=mesh, in_specs=placed, out_specs=P("ba", ("aa", "col")), check_vma=False
    )
```

```python
import functools
import math

import jax
import jax.numpy as jnp
from jax import lax
from jax.experimental import pallas as pl
from jax.experimental.pallas import tpu as pltpu
from jax.sharding import PartitionSpec as P

VMEM_LIMIT = 44 << 20
BRIEF = pl.CostEstimate(flops=0, bytes_accessed=0, transcendentals=0)
LAG = 2
DEEP = 2
PASS = 5
AHEAD = 1
ORDERED = 1
HALF_SEND = 0
HALF_TAKE = 0
HALF_GRAM = 1
GRAM_LATE = 0
STRIPS = 3
FIRST = [1, 1, 1, 1, 1, 1]
MIDDLE = [3, 3]
LAST = [1, 2, 2, 1]
APART = 1


def swap(x, axis, bit):
    return lax.ppermute(x, axis, [(i, i ^ bit) for i in range(lax.axis_size(axis))])


def tie(x, *after):
    return lax.optimization_barrier((x, *after))[0]


def split(x):
    high = x.astype(jnp.bfloat16)
    return high, (x - high.astype(jnp.float32)).astype(jnp.bfloat16)


def product(a, b, dims):
    dot = functools.partial(lax.dot_general, dimension_numbers=(dims, ((), ())), preferred_element_type=jnp.float32)
    return dot(a[0], b[0]) + (dot(a[0], b[1]) + dot(a[1], b[0]))


def gather_kernel(layers_ref, field_ref, out_ref, held, sems):
    count = out_ref.shape[0]
    reads = [pltpu.make_async_copy(field_ref.at[layers_ref[n]], held.at[n], sems.at[0, n]) for n in range(count)]
    writes = [pltpu.make_async_copy(held.at[n], out_ref.at[n], sems.at[1, n]) for n in range(count)]
    for read in reads:
        read.start()
    for read, write in zip(reads, writes):
        read.wait()
        write.start()
    for write in writes:
        write.wait()


def gathered(layers, field):
    shape = (layers.shape[0], *field.shape[1:])
    return pl.pallas_call(
        gather_kernel,
        in_specs=[pl.BlockSpec(memory_space=pltpu.SMEM), pl.BlockSpec(memory_space=pl.ANY)],
        out_specs=pl.BlockSpec(memory_space=pl.ANY),
        out_shape=jax.ShapeDtypeStruct(shape, field.dtype),
        scratch_shapes=[pltpu.VMEM(shape, field.dtype), pltpu.SemaphoreType.DMA((2, shape[0]))],
        compiler_params=pltpu.CompilerParams(vmem_limit_bytes=VMEM_LIMIT),
        cost_estimate=BRIEF,
    )(layers, field)


def truncate_kernel(cuts, sizes, _, *refs):
    own, came, own_factor, came_factor = refs[:4]
    layer = jnp.concatenate([own[0], came[0]], axis=0)
    factor = jnp.concatenate([own_factor[...], came_factor[...]], axis=0)
    out = product(split(layer), split(factor), ((0,), (0,)))
    owners = refs[4].shape[1]
    out = out.reshape(owners, -1, out.shape[1])
    first = 0
    for part, size in enumerate(sizes):
        outs = refs[4 + part * len(cuts) : 4 + (part + 1) * len(cuts)]

        @pl.when((pl.program_id(0) >= first) & (pl.program_id(0) < first + size))
        def _():
            for ref, (low, high) in zip(outs, cuts):
                ref[0] = out[:, low:high]

        first += size


def truncated(sizes, layers, slots, field, came, factors, owners, cuts):
    count = layers.shape[0]
    _, rows, width = field.shape
    ranks = factors[0].shape[1]
    shapes = [(owners, high - low, ranks) for low, high in cuts]
    out_specs, out_shape = [], []
    for part, size in enumerate(sizes):
        first = sum(sizes[:part])
        place = functools.partial(lambda first, last, i, n: (jnp.clip(i - first, 0, last), 0, 0, 0), first, size - 1)
        out_specs += [pl.BlockSpec((1, *x), place) for x in shapes]
        out_shape += [jax.ShapeDtypeStruct((size, *x), jnp.float32) for x in shapes]
    outs = pl.pallas_call(
        functools.partial(truncate_kernel, cuts, sizes),
        grid_spec=pltpu.PrefetchScalarGridSpec(
            num_scalar_prefetch=1,
            grid=(count,),
            in_specs=[
                pl.BlockSpec((1, rows, width), lambda i, n: (n[i], 0, 0)),
                pl.BlockSpec((1, rows, width), lambda i, n: (n[count + i], 0, 0)),
                pl.BlockSpec((rows, ranks), lambda i, n: (0, 0)),
                pl.BlockSpec((rows, ranks), lambda i, n: (0, 0)),
            ],
            out_specs=out_specs,
        ),
        out_shape=out_shape,
        compiler_params=pltpu.CompilerParams(vmem_limit_bytes=VMEM_LIMIT),
        cost_estimate=BRIEF,
    )(jnp.concatenate([layers, slots]), field, came, *factors)
    return [outs[part * len(cuts) : (part + 1) * len(cuts)] for part in range(len(sizes))]


def gram_kernel(ba, widths, counts, unit, added, me_ref, *refs):
    strips, total = len(widths), ba * sum(counts)
    pieces, out_ref = refs[:total], refs[-1]
    old_ref = refs[total] if added else None
    owners, ranks = pieces[0].shape[1], pieces[0].shape[3]

    def pair(d, i):
        first = d * sum(counts) + sum(counts[:i])
        found = []
        for piece in pieces[first : first + counts[i]]:
            found += [split(piece[k].reshape(owners * widths[i], ranks)) for k in range(piece.shape[0])]
        return tuple(jnp.concatenate([x[n] for x in found], axis=1) for n in range(2))

    def put(block, row, size, value):
        value = value.reshape(owners, size, owners * unit)
        if added:
            value = value + old_ref[block, :, row : row + size, :]
        out_ref[block, :, row : row + size, :] = value

    pairs = {(d, i): pair(d, i) for d in range(ba) for i in range(strips)}
    lanes, wide = owners * unit, widths[-1]
    for d in range(ba):
        block = me_ref[0] ^ d
        row = 0
        for i, w in enumerate(widths):
            got = product(pairs[d, strips - 1], pairs[0, i], ((1,), (1,)))
            for n in range(w // unit):
                put(block, row, wide, got[:, n * lanes : (n + 1) * lanes])
                row += wide
        for n in range(wide // unit):
            mine = tuple(x[n * lanes : (n + 1) * lanes, :] for x in pairs[0, strips - 1])
            for i, w in enumerate(widths[:-1]):
                put(block, row, w, product(pairs[d, i], mine, ((1,), (1,))))
                row += w


def gram_strip(me, pieces, widths, unit, old):
    ba, counts = len(pieces), [len(x) for x in pieces[0]]
    owners, ranks = pieces[0][0][0].shape[1], pieces[0][0][0].shape[3]
    rows = (sum(widths) * widths[-1] + sum(widths[:-1]) * widths[-1]) // unit
    flat = [x for by_strip in pieces for by_chunk in by_strip for x in by_chunk]
    inner = ranks * sum(x.shape[0] for x in pieces[0][0])
    olds = [] if old is None else [old]
    full = pl.BlockSpec(memory_space=pltpu.VMEM)
    return pl.pallas_call(
        functools.partial(gram_kernel, ba, widths, counts, unit, len(olds)),
        in_specs=[pl.BlockSpec(memory_space=pltpu.SMEM)] + [full] * (len(flat) + len(olds)),
        out_specs=full,
        out_shape=jax.ShapeDtypeStruct((ba, owners, rows, owners * unit), jnp.float32),
        input_output_aliases={1 + len(flat): 0} if olds else {},
        compiler_params=pltpu.CompilerParams(vmem_limit_bytes=VMEM_LIMIT),
        cost_estimate=BRIEF,
    )(me.reshape(1).astype(jnp.int32), *flat, *olds)


def order_of(bits):
    if not bits:
        return [0]
    rest = order_of(bits[1:])
    return [d | bits[0] for d in rest] + rest


def strips_of(rest):
    if rest % 32:
        return [rest]
    return [rest // 2, rest // 4, rest // 4] if STRIPS == 3 else [rest - rest // 4, rest // 4] if STRIPS == 2 else [rest // 2, rest // 2]


def summed_over_core(region):
    aa = region.shape[0]
    core = lax.axis_index("aa") & 1
    pairs = region.reshape(aa // 2, 2, *region.shape[1:])
    send = lax.dynamic_index_in_dim(pairs, core ^ 1, 1, keepdims=False)
    return lax.dynamic_index_in_dim(pairs, core, 1, keepdims=False) + swap(send, "aa", 1)


def block_by_permutes(t):
    me_x, me_c = lax.axis_index("aa") >> 1, lax.axis_index("col")
    bit = t.shape[1] // 2
    while bit:
        halves = t.reshape(t.shape[0], 2, bit, *t.shape[2:])
        side = (me_c // bit) & 1
        leaving = lax.dynamic_index_in_dim(halves, side ^ 1, 1, keepdims=False)
        t = lax.dynamic_index_in_dim(halves, side, 1, keepdims=False) + swap(leaving, "col", bit)
        bit //= 2
    total = t[:, 0]
    places = total.shape[0]
    mine = lax.dynamic_index_in_dim(total, me_x, 0, keepdims=False)
    for d in range(1, places):
        mine = mine + swap(lax.dynamic_index_in_dim(total, me_x ^ d, 0, keepdims=False), "aa", 2 * d)
    return mine


def block_by_all_to_all(t):
    aa, col = 2 * t.shape[0], t.shape[1]
    groups = [[(x * 2 + c) * col + z for x in range(aa // 2) for z in range(col)] for c in range(2)]
    t = t.reshape(aa // 2 * col, *t.shape[2:])
    return jnp.sum(lax.all_to_all(t, ("aa", "col"), 0, 0, tiled=True, axis_index_groups=groups), axis=0)


def shards(field, factor):
    aa, ba, col = (lax.axis_size(n) for n in ("aa", "ba", "col"))
    me_a, me_b = lax.axis_index("aa"), lax.axis_index("ba")
    ranks, width = factor.shape[1], field.shape[2]
    depth = field.shape[0] * col
    each = field.shape[0] // aa
    rest = ba * width // (aa * col)
    owners = width // rest
    widths = strips_of(rest)
    unit = widths[-1]
    bits = [1 << n for n in range(aa.bit_length() - 1)]
    keep = order_of(bits[1:])
    middle = each // 2
    halves = [range(middle), range(middle, each)] if middle else [range(each)]

    def groups_of(i):
        sizes = [1] * each if each != 6 else FIRST if i == 0 else LAST if i == len(widths) - 1 else MIDDLE
        if each != 6 and i:
            sizes = [len(x) for x in halves]
        return [range(sum(sizes[:n]), sum(sizes[: n + 1])) for n in range(len(sizes))]

    cuts = [(0, widths[0])] + ([(widths[0], rest)] if len(widths) > 1 else [])
    trips = [range(c, c + 1) for c in range(min(2, each))] + ([range(2, each)] if each > 2 else [])
    came_of, terms = {}, {}
    factors = [factor, swap(factor, "aa", 1)]
    for n, trip in enumerate(trips):
        first = (me_a & 1 ^ 1) * each
        if n:
            first = tie(first, going, *(factors[1:] if n == 1 else []))
        going = gathered(jnp.stack([first + 2 * each * x + c for x in range(aa // 2) for c in trip]), field)
        if n > 1:
            going = tie(going, came_of[0][0])
        came = swap(going, "aa", 1)
        for c in trip:
            came_of[c] = came, [(me_a ^ d) // 2 * len(trip) + c - trip[0] for d in keep]

    def truncate(c, *after):
        came, slots = came_of[c]
        half = len(keep) // 2
        parts = [x for x in (range(half), range(half, len(keep))) if x]
        terms[c] = []
        for together in [[x] for x in parts] if c < APART else [parts]:
            layers = jnp.stack([(me_a ^ keep[n]) * each + c for part in together for n in part])
            places = jnp.stack([slots[n] for part in together for n in part])
            sizes = [len(x) for x in together]
            terms[c] += truncated(sizes, tie(layers, *after), places, field, came, factors, owners, cuts)
            after = terms[c][-1][:1]

    def terms_of(part, group, i):
        cut = min(i, 1)
        first = sum(widths[:i]) - cuts[cut][0]
        found = [terms[c][part][cut] for c in group]
        found = [x.reshape(x.shape[0], 1, *x.shape[1:])[:, :, :, first : first + widths[i]] for x in found]
        return jnp.concatenate(found, axis=1)

    steps = [(i, group) for i in range(len(widths)) for group in groups_of(i)]
    pieces = {}
    regions, blocks = [None] * len(widths), []
    arrived, passed, waiting, halfway, leaving_of = [], [], [], [], {}

    def add_gram(i, group, *after):
        used = [
            [[pieces[d, s, g] for g in groups_of(s) if g[0] in group] for s in range(i + 1)] for d in range(ba)
        ]
        regions[i] = gram_strip(tie(me_b, *after, *halfway[:HALF_GRAM]), used, widths[: i + 1], unit, regions[i])
        if group[-1] == each - 1:
            region = regions[i].reshape(aa, col, *regions[i].shape[2:])
            summed = summed_over_core(region)
            halfway.append(summed)
            blocks.append(block_by_permutes(summed) if i < len(widths) - 1 else block_by_all_to_all(summed))

    def send(n):
        i, group = steps[n]
        if i == 0:
            for c in group:
                truncate(c, *(terms[c - 1][-1][:1] if c else []), *(arrived[n - DEEP : n - DEEP + 1] if n >= DEEP else []))
        after = ([arrived[n - DEEP]] if n >= DEEP else []) + (passed[n - PASS] if n >= PASS else []) + halfway[:HALF_SEND]
        leaving_of[n] = terms_of(0, group, i)
        if after:
            leaving_of[n] = tie(leaving_of[n], *after)

    for n in range(min(DEEP - 1, len(steps))):
        send(n)
    for n, (i, group) in enumerate(steps):
        ahead = n + DEEP - 1
        if ahead < len(steps):
            send(ahead)
        leaving = leaving_of[n]
        late = min(n + AHEAD, len(steps) - 1, len(leaving_of) - 1)
        t = tie(terms_of(-1, group, i), leaving_of[late], *arrived[len(arrived) - ORDERED :], *halfway[:HALF_TAKE])
        for bit in bits[1:]:
            t = t + swap(leaving, "aa", bit)
            half = t.shape[0] // 2
            leaving, t = (t[:half], t[half:]) if half else (t, t)
        t = t[0]
        arrived.append(t)
        passed.append([swap(t, "ba", d) for d in range(1, ba)])
        for d, x in enumerate([t] + passed[-1]):
            pieces[d, i, group] = x
        for part in halves:
            if group[-1] == part[-1]:
                waiting.append((n, i, part))
        if waiting and waiting[0][0] <= n - LAG:
            add_gram(*waiting.pop(0)[1:], t if GRAM_LATE else leaving_of[min(ahead, len(steps) - 1)])
    while waiting:
        add_gram(*waiting.pop(0)[1:])

    lanes = owners * unit
    columns = [[None] * len(widths) for _ in widths]
    for j, wide in enumerate(widths):
        row = 0
        for i in range(j + 1):
            n = widths[i] // unit
            columns[i][j] = blocks[j][row : row + n * wide].reshape(n, wide, lanes).swapaxes(1, 2).reshape(n * lanes, wide)
            row += n * wide
        n, before = wide // unit, sum(widths[:j])
        if j:
            earlier = blocks[j][row:].reshape(n, before, lanes).swapaxes(1, 2).reshape(n * lanes, before)
            for i in range(j):
                at = sum(widths[:i])
                columns[j][i] = earlier[:, at : at + widths[i]]
    parts = [jnp.concatenate(columns[i], axis=1).reshape(owners, widths[i], rest) for i in range(len(widths))]
    return jnp.concatenate(parts, axis=1).reshape(width, rest) / jnp.sqrt(jnp.float32(ranks * depth))


def solution(mesh):
    placed = (P("col", "aa", "ba"), P("aa", None))
    return jax.shard_map(
        shards, mesh=mesh, in_specs=placed, out_specs=P("ba", ("aa", "col")), check_vma=False
    )
```

```python
import functools
import math

import jax
import jax.numpy as jnp
from jax import lax
from jax.experimental import pallas as pl
from jax.experimental.pallas import tpu as pltpu
from jax.sharding import PartitionSpec as P

VMEM_LIMIT = 44 << 20
BRIEF = pl.CostEstimate(flops=0, bytes_accessed=0, transcendentals=0)
DEEP = 2
LAG = 2


def swap(x, axis, bit):
    return lax.ppermute(x, axis, [(i, i ^ bit) for i in range(lax.axis_size(axis))])


def tie(x, *after):
    return lax.optimization_barrier((x, *after))[0]


def split(x):
    high = x.astype(jnp.bfloat16)
    return high, (x - high.astype(jnp.float32)).astype(jnp.bfloat16)


def product(a, b, dims):
    dot = functools.partial(lax.dot_general, dimension_numbers=(dims, ((), ())), preferred_element_type=jnp.float32)
    return dot(a[0], b[0]) + (dot(a[0], b[1]) + dot(a[1], b[0]))


def gather_kernel(layers_ref, field_ref, out_ref, held, sems):
    count = out_ref.shape[0]
    reads = [pltpu.make_async_copy(field_ref.at[layers_ref[n]], held.at[n], sems.at[0, n]) for n in range(count)]
    writes = [pltpu.make_async_copy(held.at[n], out_ref.at[n], sems.at[1, n]) for n in range(count)]
    for read in reads:
        read.start()
    for read, write in zip(reads, writes):
        read.wait()
        write.start()
    for write in writes:
        write.wait()


def gathered(layers, field):
    shape = (layers.shape[0], *field.shape[1:])
    return pl.pallas_call(
        gather_kernel,
        in_specs=[pl.BlockSpec(memory_space=pltpu.SMEM), pl.BlockSpec(memory_space=pl.ANY)],
        out_specs=pl.BlockSpec(memory_space=pl.ANY),
        out_shape=jax.ShapeDtypeStruct(shape, field.dtype),
        scratch_shapes=[pltpu.VMEM(shape, field.dtype), pltpu.SemaphoreType.DMA((2, shape[0]))],
        compiler_params=pltpu.CompilerParams(vmem_limit_bytes=VMEM_LIMIT),
        cost_estimate=BRIEF,
    )(layers, field)


def truncate_kernel(cuts, sizes, _, *refs):
    own, came, own_factor, came_factor = refs[:4]
    layer = jnp.concatenate([own[0], came[0]], axis=0)
    factor = jnp.concatenate([own_factor[...], came_factor[...]], axis=0)
    out = product(split(layer), split(factor), ((0,), (0,)))
    owners = refs[4].shape[1]
    out = out.reshape(owners, -1, out.shape[1])
    first = 0
    for part, size in enumerate(sizes):
        outs = refs[4 + part * len(cuts) : 4 + (part + 1) * len(cuts)]

        @pl.when((pl.program_id(0) >= first) & (pl.program_id(0) < first + size))
        def _():
            for ref, (low, high) in zip(outs, cuts):
                ref[0] = out[:, low:high]

        first += size


def truncated(sizes, layers, slots, field, came, factors, owners, cuts):
    count = layers.shape[0]
    _, rows, width = field.shape
    ranks = factors[0].shape[1]
    shapes = [(owners, high - low, ranks) for low, high in cuts]
    out_specs, out_shape = [], []
    for part, size in enumerate(sizes):
        first = sum(sizes[:part])
        place = functools.partial(lambda first, last, i, n: (jnp.clip(i - first, 0, last), 0, 0, 0), first, size - 1)
        out_specs += [pl.BlockSpec((1, *x), place) for x in shapes]
        out_shape += [jax.ShapeDtypeStruct((size, *x), jnp.float32) for x in shapes]
    outs = pl.pallas_call(
        functools.partial(truncate_kernel, cuts, sizes),
        grid_spec=pltpu.PrefetchScalarGridSpec(
            num_scalar_prefetch=1,
            grid=(count,),
            in_specs=[
                pl.BlockSpec((1, rows, width), lambda i, n: (n[i], 0, 0)),
                pl.BlockSpec((1, rows, width), lambda i, n: (n[count + i], 0, 0)),
                pl.BlockSpec((rows, ranks), lambda i, n: (0, 0)),
                pl.BlockSpec((rows, ranks), lambda i, n: (0, 0)),
            ],
            out_specs=out_specs,
        ),
        out_shape=out_shape,
        compiler_params=pltpu.CompilerParams(vmem_limit_bytes=VMEM_LIMIT),
        cost_estimate=BRIEF,
    )(jnp.concatenate([layers, slots]), field, came, *factors)
    return [outs[part * len(cuts) : (part + 1) * len(cuts)] for part in range(len(sizes))]


def gram_kernel(ba, widths, counts, unit, added, me_ref, *refs):
    strips, total = len(widths), ba * sum(counts)
    pieces, out_ref = refs[:total], refs[-1]
    old_ref = refs[total] if added else None
    owners, ranks = pieces[0].shape[1], pieces[0].shape[3]

    def pair(d, i):
        first = d * sum(counts) + sum(counts[:i])
        found = []
        for piece in pieces[first : first + counts[i]]:
            found += [split(piece[k].reshape(owners * widths[i], ranks)) for k in range(piece.shape[0])]
        return tuple(jnp.concatenate([x[n] for x in found], axis=1) for n in range(2))

    def put(block, row, size, value):
        value = value.reshape(owners, size, owners * unit)
        if added:
            value = value + old_ref[block, :, row : row + size, :]
        out_ref[block, :, row : row + size, :] = value

    pairs = {(d, i): pair(d, i) for d in range(ba) for i in range(strips)}
    lanes, wide = owners * unit, widths[-1]
    for d in range(ba):
        block = me_ref[0] ^ d
        row = 0
        for i, w in enumerate(widths):
            got = product(pairs[d, strips - 1], pairs[0, i], ((1,), (1,)))
            for n in range(w // unit):
                put(block, row, wide, got[:, n * lanes : (n + 1) * lanes])
                row += wide
        for n in range(wide // unit):
            mine = tuple(x[n * lanes : (n + 1) * lanes, :] for x in pairs[0, strips - 1])
            for i, w in enumerate(widths[:-1]):
                put(block, row, w, product(pairs[d, i], mine, ((1,), (1,))))
                row += w


def gram_strip(me, pieces, widths, unit, old):
    ba, counts = len(pieces), [len(x) for x in pieces[0]]
    owners, ranks = pieces[0][0][0].shape[1], pieces[0][0][0].shape[3]
    rows = (sum(widths) * widths[-1] + sum(widths[:-1]) * widths[-1]) // unit
    flat = [x for by_strip in pieces for by_chunk in by_strip for x in by_chunk]
    inner = ranks * sum(x.shape[0] for x in pieces[0][0])
    olds = [] if old is None else [old]
    full = pl.BlockSpec(memory_space=pltpu.VMEM)
    return pl.pallas_call(
        functools.partial(gram_kernel, ba, widths, counts, unit, len(olds)),
        in_specs=[pl.BlockSpec(memory_space=pltpu.SMEM)] + [full] * (len(flat) + len(olds)),
        out_specs=full,
        out_shape=jax.ShapeDtypeStruct((ba, owners, rows, owners * unit), jnp.float32),
        input_output_aliases={1 + len(flat): 0} if olds else {},
        compiler_params=pltpu.CompilerParams(vmem_limit_bytes=VMEM_LIMIT),
        cost_estimate=BRIEF,
    )(me.reshape(1).astype(jnp.int32), *flat, *olds)


def order_of(bits):
    if not bits:
        return [0]
    rest = order_of(bits[1:])
    return [d | bits[0] for d in rest] + rest


def strips_of(rest):
    return [rest // 2, rest // 4, rest // 4] if rest % 32 == 0 else [rest]


def summed_over_core(region):
    aa = region.shape[0]
    core = lax.axis_index("aa") & 1
    pairs = region.reshape(aa // 2, 2, *region.shape[1:])
    send = lax.dynamic_index_in_dim(pairs, core ^ 1, 1, keepdims=False)
    return lax.dynamic_index_in_dim(pairs, core, 1, keepdims=False) + swap(send, "aa", 1)


def block_by_permutes(t):
    me_x, me_c = lax.axis_index("aa") >> 1, lax.axis_index("col")
    bit = t.shape[1] // 2
    while bit:
        halves = t.reshape(t.shape[0], 2, bit, *t.shape[2:])
        side = (me_c // bit) & 1
        leaving = lax.dynamic_index_in_dim(halves, side ^ 1, 1, keepdims=False)
        t = lax.dynamic_index_in_dim(halves, side, 1, keepdims=False) + swap(leaving, "col", bit)
        bit //= 2
    total = t[:, 0]
    places = total.shape[0]
    mine = lax.dynamic_index_in_dim(total, me_x, 0, keepdims=False)
    for d in range(1, places):
        mine = mine + swap(lax.dynamic_index_in_dim(total, me_x ^ d, 0, keepdims=False), "aa", 2 * d)
    return mine


def block_by_all_to_all(t):
    aa, col = 2 * t.shape[0], t.shape[1]
    groups = [[(x * 2 + c) * col + z for x in range(aa // 2) for z in range(col)] for c in range(2)]
    t = t.reshape(aa // 2 * col, *t.shape[2:])
    return jnp.sum(lax.all_to_all(t, ("aa", "col"), 0, 0, tiled=True, axis_index_groups=groups), axis=0)


def shards(field, factor):
    aa, ba, col = (lax.axis_size(n) for n in ("aa", "ba", "col"))
    me_a, me_b = lax.axis_index("aa"), lax.axis_index("ba")
    ranks, width = factor.shape[1], field.shape[2]
    depth = field.shape[0] * col
    each = field.shape[0] // aa
    rest = ba * width // (aa * col)
    owners = width // rest
    widths = strips_of(rest)
    unit = widths[-1]
    bits = [1 << n for n in range(aa.bit_length() - 1)]
    keep = order_of(bits[1:])
    middle = each // 2
    halves = [range(middle), range(middle, each)] if middle else [range(each)]

    def groups_of(i):
        if i == 0:
            return [range(c, c + 1) for c in range(each)]
        if i == len(widths) - 1 and len(halves) == 2 and middle > 1:
            cuts = [0, 1, middle, each - 1, each]
            return [range(low, high) for low, high in zip(cuts, cuts[1:])]
        return halves

    cuts = [(0, widths[0])] + ([(widths[0], rest)] if len(widths) > 1 else [])
    trips = [range(c, c + 1) for c in range(min(2, each))] + ([range(2, each)] if each > 2 else [])
    came_of, terms = {}, {}
    factors = [factor, swap(factor, "aa", 1)]
    def exchange(*after):
        trip = trips.pop(0)
        first = (me_a & 1 ^ 1) * each
        first = tie(first, *after) if after else first
        going = gathered(jnp.stack([first + 2 * each * x + c for x in range(aa // 2) for c in trip]), field)
        if len(came_of) > 1:
            going = tie(going, came_of[0][0])
        came = swap(going, "aa", 1)
        for c in trip:
            came_of[c] = came, [(me_a ^ d) // 2 * len(trip) + c - trip[0] for d in keep]
        return going

    def truncate(c, *after):
        came, slots = came_of[c]
        half = len(keep) // 2
        parts = [x for x in (range(half), range(half, len(keep))) if x]
        terms[c] = []
        for together in [parts] if c else [[x] for x in parts]:
            layers = jnp.stack([(me_a ^ keep[n]) * each + c for part in together for n in part])
            places = jnp.stack([slots[n] for part in together for n in part])
            sizes = [len(x) for x in together]
            terms[c] += truncated(sizes, tie(layers, *after), places, field, came, factors, owners, cuts)
            after = terms[c][-1][:1]
            if c == 0 and trips:
                exchange(*after)
        while c == 0 and trips:
            exchange(*after)

    def terms_of(part, group, i):
        cut = min(i, 1)
        first = sum(widths[:i]) - cuts[cut][0]
        found = [terms[c][part][cut] for c in group]
        found = [x.reshape(x.shape[0], 1, *x.shape[1:])[:, :, :, first : first + widths[i]] for x in found]
        return jnp.concatenate(found, axis=1)

    steps = [(i, group) for i in range(len(widths)) for group in groups_of(i)]
    pieces = {}
    regions, blocks = [None] * len(widths), []
    arrived, passed, waiting, halfway, leaving_of = [], [], [], [], {}

    def add_gram(i, group, *after):
        used = [
            [[pieces[d, s, g] for g in groups_of(s) if g[0] in group] for s in range(i + 1)] for d in range(ba)
        ]
        regions[i] = gram_strip(tie(me_b, *after, *halfway[:1]), used, widths[: i + 1], unit, regions[i])
        if group[-1] == each - 1:
            region = regions[i].reshape(aa, col, *regions[i].shape[2:])
            summed = summed_over_core(region)
            halfway.append(summed)
            blocks.append(block_by_permutes(summed) if i < len(widths) - 1 else block_by_all_to_all(summed))

    def send(n):
        i, group = steps[n]
        if i == 0:
            for c in group:
                truncate(c, *(terms[c - 1][-1][:1] if c else [first]), *arrived[max(n - DEEP, 0) : max(n - DEEP + 1, 0)])
        after = arrived[max(n - DEEP, 0) : max(n - DEEP + 1, 0)] + (passed[n - DEEP - 3] if n >= DEEP + 3 else [])
        leaving_of[n] = terms_of(0, group, i)
        if after:
            leaving_of[n] = tie(leaving_of[n], *after)

    first = exchange()
    for n in range(min(DEEP - 1, len(steps))):
        send(n)
    for n, (i, group) in enumerate(steps):
        ahead = n + DEEP - 1
        if ahead < len(steps):
            send(ahead)
        leaving = leaving_of[n]
        t = tie(terms_of(-1, group, i), leaving_of[min(ahead, len(steps) - 1)], *arrived[-1:])
        for bit in bits[1:]:
            t = t + swap(leaving, "aa", bit)
            half = t.shape[0] // 2
            leaving, t = (t[:half], t[half:]) if half else (t, t)
        t = t[0]
        arrived.append(t)
        passed.append([swap(t, "ba", d) for d in range(1, ba)])
        for d, x in enumerate([t] + passed[-1]):
            pieces[d, i, group] = x
        for part in halves:
            if group[-1] == part[-1]:
                waiting.append((n, i, part))
        if waiting and waiting[0][0] <= n - LAG:
            add_gram(*waiting.pop(0)[1:], leaving_of[min(ahead, len(steps) - 1)])
    while waiting:
        add_gram(*waiting.pop(0)[1:])

    lanes = owners * unit
    columns = [[None] * len(widths) for _ in widths]
    for j, wide in enumerate(widths):
        row = 0
        for i in range(j + 1):
            n = widths[i] // unit
            columns[i][j] = blocks[j][row : row + n * wide].reshape(n, wide, lanes).swapaxes(1, 2).reshape(n * lanes, wide)
            row += n * wide
        n, before = wide // unit, sum(widths[:j])
        if j:
            earlier = blocks[j][row:].reshape(n, before, lanes).swapaxes(1, 2).reshape(n * lanes, before)
            for i in range(j):
                at = sum(widths[:i])
                columns[j][i] = earlier[:, at : at + widths[i]]
    parts = [jnp.concatenate(columns[i], axis=1).reshape(owners, widths[i], rest) for i in range(len(widths))]
    return jnp.concatenate(parts, axis=1).reshape(width, rest) / jnp.sqrt(jnp.float32(ranks * depth))


def solution(mesh):
    placed = (P("col", "aa", "ba"), P("aa", None))
    return jax.shard_map(
        shards, mesh=mesh, in_specs=placed, out_specs=P("ba", ("aa", "col")), check_vma=False
    )
```

```python
import functools
import math

import jax
import jax.numpy as jnp
from jax import lax
from jax.experimental import pallas as pl
from jax.experimental.pallas import tpu as pltpu
from jax.sharding import PartitionSpec as P

VMEM_LIMIT = 44 << 20
BRIEF = pl.CostEstimate(flops=0, bytes_accessed=0, transcendentals=0)
DEEP = 2
LAG = 2


def swap(x, axis, bit):
    return lax.ppermute(x, axis, [(i, i ^ bit) for i in range(lax.axis_size(axis))])


def tie(x, *after):
    return lax.optimization_barrier((x, *after))[0]


def split(x):
    high = x.astype(jnp.bfloat16)
    return high, (x - high.astype(jnp.float32)).astype(jnp.bfloat16)


def product(a, b, dims):
    dot = functools.partial(lax.dot_general, dimension_numbers=(dims, ((), ())), preferred_element_type=jnp.float32)
    return dot(a[0], b[0]) + (dot(a[0], b[1]) + dot(a[1], b[0]))


def gather_kernel(layers_ref, field_ref, out_ref, held, sems):
    count = out_ref.shape[0]
    reads = [pltpu.make_async_copy(field_ref.at[layers_ref[n]], held.at[n], sems.at[0, n]) for n in range(count)]
    writes = [pltpu.make_async_copy(held.at[n], out_ref.at[n], sems.at[1, n]) for n in range(count)]
    for read in reads:
        read.start()
    for read, write in zip(reads, writes):
        read.wait()
        write.start()
    for write in writes:
        write.wait()


def gathered(layers, field):
    shape = (layers.shape[0], *field.shape[1:])
    return pl.pallas_call(
        gather_kernel,
        in_specs=[pl.BlockSpec(memory_space=pltpu.SMEM), pl.BlockSpec(memory_space=pl.ANY)],
        out_specs=pl.BlockSpec(memory_space=pl.ANY),
        out_shape=jax.ShapeDtypeStruct(shape, field.dtype),
        scratch_shapes=[pltpu.VMEM(shape, field.dtype), pltpu.SemaphoreType.DMA((2, shape[0]))],
        compiler_params=pltpu.CompilerParams(vmem_limit_bytes=VMEM_LIMIT),
        cost_estimate=BRIEF,
    )(layers, field)


def truncate_kernel(cuts, sizes, _, *refs):
    own, came, own_factor, came_factor = refs[:4]
    layer = jnp.concatenate([own[0], came[0]], axis=0)
    factor = jnp.concatenate([own_factor[...], came_factor[...]], axis=0)
    out = product(split(layer), split(factor), ((0,), (0,)))
    owners = refs[4].shape[1]
    out = out.reshape(owners, -1, out.shape[1])
    first = 0
    for part, size in enumerate(sizes):
        outs = refs[4 + part * len(cuts) : 4 + (part + 1) * len(cuts)]

        @pl.when((pl.program_id(0) >= first) & (pl.program_id(0) < first + size))
        def _():
            for ref, (low, high) in zip(outs, cuts):
                ref[0] = out[:, low:high]

        first += size


def truncated(sizes, layers, slots, field, came, factors, owners, cuts):
    count = layers.shape[0]
    _, rows, width = field.shape
    ranks = factors[0].shape[1]
    shapes = [(owners, high - low, ranks) for low, high in cuts]
    out_specs, out_shape = [], []
    for part, size in enumerate(sizes):
        first = sum(sizes[:part])
        place = functools.partial(lambda first, last, i, n: (jnp.clip(i - first, 0, last), 0, 0, 0), first, size - 1)
        out_specs += [pl.BlockSpec((1, *x), place) for x in shapes]
        out_shape += [jax.ShapeDtypeStruct((size, *x), jnp.float32) for x in shapes]
    outs = pl.pallas_call(
        functools.partial(truncate_kernel, cuts, sizes),
        grid_spec=pltpu.PrefetchScalarGridSpec(
            num_scalar_prefetch=1,
            grid=(count,),
            in_specs=[
                pl.BlockSpec((1, rows, width), lambda i, n: (n[i], 0, 0)),
                pl.BlockSpec((1, rows, width), lambda i, n: (n[count + i], 0, 0)),
                pl.BlockSpec((rows, ranks), lambda i, n: (0, 0)),
                pl.BlockSpec((rows, ranks), lambda i, n: (0, 0)),
            ],
            out_specs=out_specs,
        ),
        out_shape=out_shape,
        compiler_params=pltpu.CompilerParams(vmem_limit_bytes=VMEM_LIMIT),
        cost_estimate=BRIEF,
    )(jnp.concatenate([layers, slots]), field, came, *factors)
    return [outs[part * len(cuts) : (part + 1) * len(cuts)] for part in range(len(sizes))]


def gram_kernel(ba, widths, counts, unit, added, me_ref, *refs):
    strips, total = len(widths), ba * sum(counts)
    pieces, out_ref = refs[:total], refs[-1]
    old_ref = refs[total] if added else None
    owners, ranks = pieces[0].shape[1], pieces[0].shape[3]

    def pair(d, i):
        first = d * sum(counts) + sum(counts[:i])
        found = []
        for piece in pieces[first : first + counts[i]]:
            found += [split(piece[k].reshape(owners * widths[i], ranks)) for k in range(piece.shape[0])]
        return tuple(jnp.concatenate([x[n] for x in found], axis=1) for n in range(2))

    def put(block, row, size, value):
        value = value.reshape(owners, size, owners * unit)
        if added:
            value = value + old_ref[block, :, row : row + size, :]
        out_ref[block, :, row : row + size, :] = value

    pairs = {(d, i): pair(d, i) for d in range(ba) for i in range(strips)}
    lanes, wide = owners * unit, widths[-1]
    for d in range(ba):
        block = me_ref[0] ^ d
        row = 0
        for i, w in enumerate(widths):
            got = product(pairs[d, strips - 1], pairs[0, i], ((1,), (1,)))
            for n in range(w // unit):
                put(block, row, wide, got[:, n * lanes : (n + 1) * lanes])
                row += wide
        for n in range(wide // unit):
            mine = tuple(x[n * lanes : (n + 1) * lanes, :] for x in pairs[0, strips - 1])
            for i, w in enumerate(widths[:-1]):
                put(block, row, w, product(pairs[d, i], mine, ((1,), (1,))))
                row += w


def gram_strip(me, pieces, widths, unit, old):
    ba, counts = len(pieces), [len(x) for x in pieces[0]]
    owners, ranks = pieces[0][0][0].shape[1], pieces[0][0][0].shape[3]
    rows = (sum(widths) * widths[-1] + sum(widths[:-1]) * widths[-1]) // unit
    flat = [x for by_strip in pieces for by_chunk in by_strip for x in by_chunk]
    inner = ranks * sum(x.shape[0] for x in pieces[0][0])
    olds = [] if old is None else [old]
    full = pl.BlockSpec(memory_space=pltpu.VMEM)
    return pl.pallas_call(
        functools.partial(gram_kernel, ba, widths, counts, unit, len(olds)),
        in_specs=[pl.BlockSpec(memory_space=pltpu.SMEM)] + [full] * (len(flat) + len(olds)),
        out_specs=full,
        out_shape=jax.ShapeDtypeStruct((ba, owners, rows, owners * unit), jnp.float32),
        input_output_aliases={1 + len(flat): 0} if olds else {},
        compiler_params=pltpu.CompilerParams(vmem_limit_bytes=VMEM_LIMIT),
        cost_estimate=BRIEF,
    )(me.reshape(1).astype(jnp.int32), *flat, *olds)


def order_of(bits):
    if not bits:
        return [0]
    rest = order_of(bits[1:])
    return [d | bits[0] for d in rest] + rest


def strips_of(rest):
    return [rest // 2, rest // 4, rest // 4] if rest % 32 == 0 else [rest]


def summed_over_core(region):
    aa = region.shape[0]
    core = lax.axis_index("aa") & 1
    pairs = region.reshape(aa // 2, 2, *region.shape[1:])
    send = lax.dynamic_index_in_dim(pairs, core ^ 1, 1, keepdims=False)
    return lax.dynamic_index_in_dim(pairs, core, 1, keepdims=False) + swap(send, "aa", 1)


def block_by_permutes(t):
    me_x, me_c = lax.axis_index("aa") >> 1, lax.axis_index("col")
    bit = t.shape[1] // 2
    while bit:
        halves = t.reshape(t.shape[0], 2, bit, *t.shape[2:])
        side = (me_c // bit) & 1
        leaving = lax.dynamic_index_in_dim(halves, side ^ 1, 1, keepdims=False)
        t = lax.dynamic_index_in_dim(halves, side, 1, keepdims=False) + swap(leaving, "col", bit)
        bit //= 2
    return t[:, 0]


def block_over_x(total):
    me_x = lax.axis_index("aa") >> 1
    mine = lax.dynamic_index_in_dim(total, me_x, 0, keepdims=False)
    for d in range(1, total.shape[0]):
        mine = mine + swap(lax.dynamic_index_in_dim(total, me_x ^ d, 0, keepdims=False), "aa", 2 * d)
    return mine


def block_by_all_to_all(t):
    aa, col = 2 * t.shape[0], t.shape[1]
    groups = [[(x * 2 + c) * col + z for x in range(aa // 2) for z in range(col)] for c in range(2)]
    t = t.reshape(aa // 2 * col, *t.shape[2:])
    return jnp.sum(lax.all_to_all(t, ("aa", "col"), 0, 0, tiled=True, axis_index_groups=groups), axis=0)


def shards(field, factor):
    aa, ba, col = (lax.axis_size(n) for n in ("aa", "ba", "col"))
    me_a, me_b = lax.axis_index("aa"), lax.axis_index("ba")
    ranks, width = factor.shape[1], field.shape[2]
    depth = field.shape[0] * col
    each = field.shape[0] // aa
    rest = ba * width // (aa * col)
    owners = width // rest
    widths = strips_of(rest)
    unit = widths[-1]
    bits = [1 << n for n in range(aa.bit_length() - 1)]
    keep = order_of(bits[1:])
    middle = each // 2
    halves = [range(middle), range(middle, each)] if middle else [range(each)]

    def groups_of(i):
        if i == 0:
            return [range(c, c + 1) for c in range(each)]
        if i == len(widths) - 1 and len(halves) == 2 and middle > 1:
            cuts = [0, 1, middle, each - 1, each]
            return [range(low, high) for low, high in zip(cuts, cuts[1:])]
        return halves

    cuts = [(0, widths[0])] + ([(widths[0], rest)] if len(widths) > 1 else [])
    trips = [range(c, c + 1) for c in range(min(2, each))] + ([range(2, each)] if each > 2 else [])
    came_of, terms = {}, {}
    factors = [factor, swap(factor, "aa", 1)]
    def exchange(*after):
        trip = trips.pop(0)
        first = (me_a & 1 ^ 1) * each
        first = tie(first, *after) if after else first
        going = gathered(jnp.stack([first + 2 * each * x + c for x in range(aa // 2) for c in trip]), field)
        if len(came_of) > 1:
            going = tie(going, came_of[0][0])
        came = swap(going, "aa", 1)
        for c in trip:
            came_of[c] = came, [(me_a ^ d) // 2 * len(trip) + c - trip[0] for d in keep]
        return going

    def truncate(c, *after):
        came, slots = came_of[c]
        half = len(keep) // 2
        parts = [x for x in (range(half), range(half, len(keep))) if x]
        terms[c] = []
        for together in [parts] if c else [[x] for x in parts]:
            layers = jnp.stack([(me_a ^ keep[n]) * each + c for part in together for n in part])
            places = jnp.stack([slots[n] for part in together for n in part])
            sizes = [len(x) for x in together]
            terms[c] += truncated(sizes, tie(layers, *after), places, field, came, factors, owners, cuts)
            after = terms[c][-1][:1]
            if c == 0 and trips:
                exchange(*after)
        while c == 0 and trips:
            exchange(*after)

    def terms_of(part, group, i):
        cut = min(i, 1)
        first = sum(widths[:i]) - cuts[cut][0]
        found = [terms[c][part][cut] for c in group]
        found = [x.reshape(x.shape[0], 1, *x.shape[1:])[:, :, :, first : first + widths[i]] for x in found]
        return jnp.concatenate(found, axis=1)

    steps = [(i, group) for i in range(len(widths)) for group in groups_of(i)]
    pieces = {}
    regions, blocks = [None] * len(widths), []
    arrived, passed, waiting, halfway, early, leaving_of = [], [], [], [], [], {}

    def add_gram(i, group, *after):
        used = [
            [[pieces[d, s, g] for g in groups_of(s) if g[0] in group] for s in range(i + 1)] for d in range(ba)
        ]
        regions[i] = gram_strip(tie(me_b, *after, *halfway[:1]), used, widths[: i + 1], unit, regions[i])
        if group[-1] == each - 1:
            region = regions[i].reshape(aa, col, *regions[i].shape[2:])
            summed = summed_over_core(region)
            halfway.append(summed)
            if i < len(widths) - 1:
                early.append(block_by_permutes(summed))
            if i == len(widths) - 2:
                joined = block_over_x(jnp.concatenate(early, axis=1))
                rows = [0]
                for x in early:
                    rows.append(rows[-1] + x.shape[1])
                blocks.extend(joined[low:high] for low, high in zip(rows, rows[1:]))
            if i == len(widths) - 1:
                blocks.append(block_by_all_to_all(summed))

    def send(n):
        i, group = steps[n]
        if i == 0:
            for c in group:
                truncate(c, *(terms[c - 1][-1][:1] if c else [first]), *arrived[max(n - DEEP, 0) : max(n - DEEP + 1, 0)])
        after = arrived[max(n - DEEP, 0) : max(n - DEEP + 1, 0)] + (passed[n - DEEP - 3] if n >= DEEP + 3 else [])
        leaving_of[n] = terms_of(0, group, i)
        if after:
            leaving_of[n] = tie(leaving_of[n], *after)

    first = exchange()
    for n in range(min(DEEP - 1, len(steps))):
        send(n)
    for n, (i, group) in enumerate(steps):
        ahead = n + DEEP - 1
        if ahead < len(steps):
            send(ahead)
        leaving = leaving_of[n]
        t = tie(terms_of(-1, group, i), leaving_of[min(ahead, len(steps) - 1)], *arrived[-1:])
        for bit in bits[1:]:
            t = t + swap(leaving, "aa", bit)
            half = t.shape[0] // 2
            leaving, t = (t[:half], t[half:]) if half else (t, t)
        t = t[0]
        arrived.append(t)
        passed.append([swap(t, "ba", d) for d in range(1, ba)])
        for d, x in enumerate([t] + passed[-1]):
            pieces[d, i, group] = x
        for part in halves:
            if group[-1] == part[-1]:
                waiting.append((n, i, part))
        if waiting and waiting[0][0] <= n - LAG:
            add_gram(*waiting.pop(0)[1:], leaving_of[min(ahead, len(steps) - 1)])
    while waiting:
        add_gram(*waiting.pop(0)[1:])

    lanes = owners * unit
    columns = [[None] * len(widths) for _ in widths]
    for j, wide in enumerate(widths):
        row = 0
        for i in range(j + 1):
            n = widths[i] // unit
            columns[i][j] = blocks[j][row : row + n * wide].reshape(n, wide, lanes).swapaxes(1, 2).reshape(n * lanes, wide)
            row += n * wide
        n, before = wide // unit, sum(widths[:j])
        if j:
            earlier = blocks[j][row:].reshape(n, before, lanes).swapaxes(1, 2).reshape(n * lanes, before)
            for i in range(j):
                at = sum(widths[:i])
                columns[j][i] = earlier[:, at : at + widths[i]]
    parts = [jnp.concatenate(columns[i], axis=1).reshape(owners, widths[i], rest) for i in range(len(widths))]
    return jnp.concatenate(parts, axis=1).reshape(width, rest) / jnp.sqrt(jnp.float32(ranks * depth))


def solution(mesh):
    placed = (P("col", "aa", "ba"), P("aa", None))
    return jax.shard_map(
        shards, mesh=mesh, in_specs=placed, out_specs=P("ba", ("aa", "col")), check_vma=False
    )
```
